512 devices in a mesh: row: 16 (over y, core), col: 32 (over x, z).
Axes of the slice: x: 4, y: 8, z: 8, core: 2. Of those that a mesh axis runs over, the one named last changes fastest.
Arguments:
- points: float32 [64, 32768], P(None, ('row', 'col')), may hold values from -6 to 6
- lengthscale: float32 [64], replicated, may hold values from 2 to 8
- noise: float32 [32768], P(('row', 'col')), may hold values from 0.5 to 4
- iterate: float32 [16, 32768], P(None, ('row', 'col')), may hold values from -6 to 6
- residual: float32 [16, 32768], P(None, ('row', 'col')), may hold values from -6 to 6
- direction: float32 [16, 32768], P(None, ('row', 'col')), may hold values from -6 to 6
Outputs:
- new_iterate: float32 [16, 32768], P(None, ('row', 'col'))
- new_residual: float32 [16, 32768], P(None, ('row', 'col'))
- new_direction: float32 [16, 32768], P(None, ('row', 'col'))
The draws below stay inside these ranges and needn't reach their ends.
All inputs are finite; a program needn't handle non-finite values.
Results may differ from the reference program's by a relative error of at most 0.004.
Values may be sent and summed in bfloat16 or wider, within the bound.
A program may use at most 64 MiB of HBM per device.

```python
import math
import jax
import jax.numpy as jnp
from jax import lax

FEAT = 64
RHS = 16
POINTS = 32768


def shard_levels(key, dims, shards, least, top_value):
    level = 1.0
    for dim, blocks in shards:
        steps = jax.random.uniform(jax.random.fold_in(jax.random.fold_in(key, 6), dim), (blocks,), jnp.float32, least / len(shards), top_value / len(shards))
        level = level * jnp.repeat(jnp.exp(steps), dims[dim] // blocks).reshape((-1,) + (1,) * (len(dims) - 1 - dim))
    return level


def centred(rng, extent, scale, most, pieces=(), kind=jnp.bfloat16):
    entries = jax.random.normal(rng, extent, jnp.float32) * scale
    if len(pieces) > 0:
        entries = shard_levels(rng, extent, pieces, -0.22, 0.18) * entries
    return jnp.clip(entries, min=-most, max=most).astype(kind)


def setup_inputs(seed: int = 0) -> dict:
    key_list = jax.random.split(jax.random.key(seed), 7)
    return {
        "points": centred(key_list[0], (FEAT, POINTS), 1.0, 6.0, ((1, 512),), jnp.float32),
        "lengthscale": jnp.clip(jnp.exp(jax.random.uniform(key_list[1], (FEAT,), jnp.float32, math.log(2.0), math.log(8.0))), 2.0, 8.0),
        "noise": jnp.clip(jnp.exp(math.log(4.0) - 2.0794415 * jax.random.uniform(key_list[2], (POINTS,), jnp.float32) ** shard_levels(key_list[2], (POINTS,), ((0, 512),), -0.2, 0.2)), 0.5, 4.0),
        "iterate": centred(key_list[3], (RHS, POINTS), 1.0, 6.0, ((1, 512),), jnp.float32),
        "residual": centred(key_list[4], (RHS, POINTS), 1.0, 6.0, ((1, 512),), jnp.float32),
        "direction": centred(key_list[5], (RHS, POINTS), 1.0, 6.0, ((1, 512),), jnp.float32),
    }


def matern(rows_z, cols_z):
    sq_rows = lax.optimization_barrier(jnp.sum(rows_z * rows_z, axis=0))
    sq_cols = lax.optimization_barrier(jnp.sum(cols_z * cols_z, axis=0))
    inner = lax.dot_general(rows_z, cols_z, (((0,), (0,)), ((), ())), precision=lax.Precision.HIGHEST, preferred_element_type=jnp.float32)
    dist2 = jnp.maximum(sq_rows[:, None] + sq_cols[None, :] - 2.0 * inner, 0.0)
    scaled = jnp.sqrt(5.0 * dist2)
    return ((1.0 + scaled + scaled * scaled / 3.0) * jnp.exp(-scaled)).astype(jnp.bfloat16)

def reference(points, lengthscale, noise, iterate, residual, direction):
    scaled = points / lengthscale[:, None]
    dir_half = direction.astype(jnp.bfloat16)
    feats = scaled.shape[0]
    count = scaled.shape[1]
    width = math.gcd(count, 512)
    blocks = scaled.reshape(feats, count // width, width).transpose(1, 0, 2)

    def one_block(block_z):
        kern = matern(block_z, scaled)
        return lax.dot_general(dir_half, kern, (((1,), (1,)), ((), ())), preferred_element_type=jnp.float32)
    parts = lax.map(one_block, blocks)
    image = parts.transpose(1, 0, 2).reshape(dir_half.shape[0], count)
    image = image + noise[None, :] * direction
    norm_now = lax.optimization_barrier(jnp.sum(residual * residual, axis=1))
    curv = lax.optimization_barrier(jnp.sum(direction * image, axis=1))
    alpha = norm_now / curv
    new_iterate = iterate + alpha[:, None] * direction
    new_residual = residual - alpha[:, None] * image
    norm_next = lax.optimization_barrier(jnp.sum(new_residual * new_residual, axis=1))
    new_direction = new_residual + (norm_next / norm_now)[:, None] * direction
    return (new_iterate, new_residual, new_direction)
```

```python
import functools
import math

import jax
import jax.numpy as jnp
from jax import lax
from jax.experimental import pallas as pl
from jax.experimental.pallas import tpu as pltpu
from jax.sharding import PartitionSpec as P

MESH = pl.DeviceIdType.MESH
F32 = jnp.float32
BF16 = jnp.bfloat16
FEAT = 64
RHS = 16
PTS = 64
NX = 4
LOG2E = math.log2(math.e)
SCALE = math.sqrt(5.0) * LOG2E
TINY = 1e-30


def half_lanes(shape):
    return lax.broadcasted_iota(jnp.int32, shape, 1) < 64


def swap(x):
    return pltpu.roll(x, 64, 1)


def split3(s):
    a = s.astype(BF16).astype(F32)
    b = (s - a).astype(BF16).astype(F32)
    c = (s - a - b).astype(BF16).astype(F32)
    return a, b, c


def kernel(
    nrow, ncol,
    points, scale, noise, iterate, residual, direction,
    new_iterate, new_residual, new_direction,
    cbuf, rbuf, rmat, amat, prod, psend, pbuf, stat_a, stat_b, tot_a, tot_b,
    c_send, c_recv, r_send, r_recv, p_send, p_recv, a_send, a_recv, b_send, b_recv,
):
    nz = ncol // NX
    row, col = lax.axis_index("row"), lax.axis_index("col")
    x, z = col // nz, col % nz

    def row_peer(d):
        return (lax.rem(row + d, nrow), col)

    def col_peer(dx, dz):
        return (row, lax.rem(x + dx, NX) * nz + lax.rem(z + dz, nz))

    dzs = [0]
    for k in range(1, nz // 2 + 1):
        dzs += [k] if 2 * k == nz else [k, nz - k]
    col_offsets = [(g, dx) for g in range(nz) for dx in range(NX) if (g, dx) != (0, 0)]

    barrier = pltpu.get_barrier_semaphore()
    for d in range(1, nrow):
        pl.semaphore_signal(barrier, inc=1, device_id=row_peer(d), device_id_type=MESH)
    for g, dx in reversed(col_offsets):
        pl.semaphore_signal(barrier, inc=1, device_id=col_peer(dx, dzs[g]), device_id_type=MESH)

    ls_col = jnp.transpose(jnp.broadcast_to(scale[...], (FEAT, FEAT)))
    zf = points[...] / ls_col * SCALE
    hi = zf.astype(BF16).astype(F32)
    lo = (zf - hi).astype(BF16).astype(F32)
    rbuf[0] = jnp.concatenate([hi, lo], axis=1).astype(BF16)
    sq = jnp.sum((hi + lo) * (hi + lo), axis=0, keepdims=True)
    s1, s2, s3 = split3(sq)
    one = jnp.ones_like(sq)
    ext = jnp.concatenate([s1, s2, s3, one, one, one, one * 0, one * 0], axis=0)
    pad = jnp.zeros((FEAT - 8, PTS), F32)
    hi_t = jnp.transpose(hi)
    lo_t = jnp.transpose(lo)
    ext_t = jnp.transpose(jnp.concatenate([ext, pad], axis=0))
    cbuf[0, 0, 0:64, :] = jnp.concatenate([hi_t, lo_t], axis=1).astype(BF16)
    own_dir = direction[...]
    packed = jnp.concatenate([own_dir, ext_t[0:16]], axis=1)
    lane16 = lax.broadcasted_iota(jnp.int32, (16, 128), 1)
    for a in range(1, 4):
        piece = jnp.concatenate([ext_t[16 * a:16 * a + 16], jnp.zeros((16, 64), F32)], axis=1)
        packed = jnp.where((lane16 >= 64 + 8 * a) & (lane16 < 72 + 8 * a), pltpu.roll(piece, 64 + 8 * a, 1), packed)
    cbuf[0, 0, 64:80, :] = packed.astype(BF16)

    pl.semaphore_wait(barrier, nrow - 1 + ncol - 1)

    sends = []

    def send(src, dst, ssem, rsem, peer):
        copy = pltpu.make_async_remote_copy(
            src_ref=src, dst_ref=dst, send_sem=ssem, recv_sem=rsem,
            device_id=peer, device_id_type=MESH)
        copy.start()
        sends.append(copy)

    def arrived(ref, sem):
        pltpu.make_async_copy(ref, ref, sem).wait()

    for d in range(1, nrow):
        send(rbuf.at[0], rbuf.at[d], r_send.at[d], r_recv, row_peer(d))
    for i, (g, dx) in enumerate(reversed(col_offsets)):
        send(cbuf.at[0, 0], cbuf.at[g, dx], c_send.at[i], c_recv.at[g], col_peer(dx, dzs[g]))

    arrived(rbuf.at[pl.ds(1, nrow - 1)], r_recv)
    left = half_lanes((FEAT, 128))
    sub = lax.broadcasted_iota(jnp.int32, (64, 128), 0)
    for pair in range(nrow // 2):
        c0 = rbuf[2 * pair].astype(F32)
        c1 = rbuf[2 * pair + 1].astype(F32)
        h = jnp.where(left, c0, swap(c1))
        l = jnp.where(left, swap(c0), c1)
        t1, t2, t3 = split3(jnp.sum((h + l) * (h + l), axis=0, keepdims=True))
        e = jnp.where(sub < 3, 1.0, jnp.where(sub == 3, t1, jnp.where(sub == 4, t2, jnp.where(sub == 5, t3, 0.0))))
        lanes = slice(128 * pair, 128 * pair + 128)
        h2 = (-2.0 * h).astype(BF16)
        rmat[0:64, lanes] = h2
        rmat[64:128, lanes] = h2
        rmat[128:192, lanes] = (-2.0 * l).astype(BF16)
        rmat[192:256, lanes] = e.astype(BF16)

    prod[...] = jnp.zeros_like(prod)
    npts = nrow * PTS
    width = 256
    left16 = half_lanes((16, 128))

    def group(g, carry):
        @pl.when(g == 0)
        def _():
            arrived(cbuf.at[0, pl.ds(1, NX - 1)], c_recv.at[0])

        @pl.when(g > 0)
        def _():
            arrived(cbuf.at[g], c_recv.at[g])

        dirs = []
        for dx in range(NX):
            tail = cbuf[g, dx, 64:80, :].astype(F32)
            dirs.append(tail)
            for a in range(4):
                rows = slice(64 * dx + 16 * a, 64 * dx + 16 * a + 16)
                body = cbuf[g, dx, 16 * a:16 * a + 16, :]
                amat[rows, 0:128] = body
                shifted = tail if a == 0 else pltpu.roll(tail, 128 - 8 * a, 1)
                amat[rows, 128:256] = jnp.where(left16, body.astype(F32), shifted).astype(BF16)
        dgrp = jnp.concatenate(
            [jnp.where(left16, dirs[0], swap(dirs[1])), jnp.where(left16, dirs[2], swap(dirs[3]))], axis=1).astype(BF16)
        for it in range(npts // width):
            lanes = slice(width * it, width * it + width)
            dist = jnp.dot(amat[...], rmat[:, lanes], preferred_element_type=F32)
            dist = jnp.maximum(dist, TINY)
            v = dist * lax.rsqrt(dist)
            w = v * (1.0 / (LOG2E * math.sqrt(3.0))) + math.sqrt(0.75)
            kern = ((w * w + 0.25) * jnp.exp2(-v)).astype(BF16)
            prod[:, lanes] += jnp.dot(dgrp, kern, preferred_element_type=F32)
        return carry

    lax.fori_loop(0, nz, group, 0)

    left8 = half_lanes((8, 128))
    for pair in range(nrow // 2):
        top = prod[0:8, 128 * pair:128 * pair + 128]
        bottom = prod[8:16, 128 * pair:128 * pair + 128]
        psend[2 * pair] = jnp.where(left8, top, swap(bottom))
        psend[2 * pair + 1] = jnp.where(left8, swap(top), bottom)
    for d in range(1, nrow):
        send(psend.at[d], pbuf.at[d], p_send.at[d], p_recv, row_peer(nrow - d))
    pbuf[0] = psend[0]
    res = residual[...]
    arrived(pbuf.at[pl.ds(1, nrow - 1)], p_recv)
    total = jnp.sum(pbuf[...], axis=0)
    image = jnp.concatenate([total, swap(total)], axis=0)[:, 0:64] + noise[...] * own_dir

    def norm(a, b):
        return jnp.sum(a * b, axis=1, keepdims=True)

    stats = jnp.where(
        lane16 == 0, norm(res, res),
        jnp.where(lane16 == 1, norm(own_dir, image),
                  jnp.where(lane16 == 2, norm(res, image),
                            jnp.where(lane16 == 3, norm(image, image), 0.0))))
    tot_a[...] = stats[0:8] + swap(stats[8:16])
    for d in range(1, nrow):
        send(tot_a, stat_a.at[d], a_send.at[d], a_recv, row_peer(d))
    stat_a[0] = tot_a[...]
    arrived(stat_a.at[pl.ds(1, nrow - 1)], a_recv)
    tot_b[...] = jnp.sum(stat_a[...], axis=0)
    for i, (g, dx) in enumerate(reversed(col_offsets)):
        send(tot_b, stat_b.at[g * NX + dx], b_send.at[i], b_recv, col_peer(dx, dzs[g]))
    stat_b[0] = tot_b[...]
    arrived(stat_b.at[pl.ds(1, ncol - 1)], b_recv)
    total = jnp.sum(stat_b[...], axis=0)
    total = jnp.concatenate([total, swap(total)], axis=0)
    rr, curv, cross, square = (total[:, k:k + 1] for k in range(4))
    alpha = rr / curv
    rr_new = jnp.maximum(rr - 2.0 * (alpha * cross) + alpha * (alpha * square), 0.0)
    beta = rr_new / rr
    fresh = res - alpha * image
    new_iterate[...] = iterate[...] + alpha * own_dir
    new_residual[...] = fresh
    new_direction[...] = fresh + beta * own_dir
    for copy in sends:
        copy.wait_send()


def solution(mesh):
    nrow, ncol = mesh.shape["row"], mesh.shape["col"]
    nz = ncol // NX
    spread = P(None, ("row", "col"))
    placed = (spread, P(), P(("row", "col")), spread, spread, spread)
    vmem = pl.BlockSpec(memory_space=pltpu.VMEM)
    dma = pltpu.SemaphoreType.DMA
    shape = jax.ShapeDtypeStruct((RHS, PTS), F32)

    step = pl.pallas_call(
        functools.partial(kernel, nrow, ncol),
        out_shape=(shape, shape, shape),
        in_specs=[vmem] * 6,
        out_specs=(vmem,) * 3,
        scratch_shapes=[
            pltpu.VMEM((nz, NX, 80, 128), BF16),
            pltpu.VMEM((nrow, 64, 128), BF16),
            pltpu.VMEM((256, nrow * PTS), BF16),
            pltpu.VMEM((256, 256), BF16),
            pltpu.VMEM((RHS, nrow * PTS), F32),
            pltpu.VMEM((nrow, 8, 128), F32),
            pltpu.VMEM((nrow, 8, 128), F32),
            pltpu.VMEM((nrow, 8, 128), F32),
            pltpu.VMEM((ncol, 8, 128), F32),
            pltpu.VMEM((8, 128), F32),
            pltpu.VMEM((8, 128), F32),
            dma((ncol,)), dma((nz,)), dma((nrow,)), dma,
            dma((nrow,)), dma, dma((nrow,)), dma, dma((ncol,)), dma,
        ],
        compiler_params=pltpu.CompilerParams(
            collective_id=0, has_side_effects=True, vmem_limit_bytes=32 * 1024 * 1024),
        name="cg_step",
    )

    def on_device(points, lengthscale, noise, iterate, residual, direction):
        return step(points, lengthscale.reshape(1, FEAT), noise.reshape(1, PTS), iterate, residual, direction)

    return jax.shard_map(
        on_device, mesh=mesh, in_specs=placed, out_specs=(spread, spread, spread), check_vma=False)
```

```python
import functools
import math

import jax
import jax.numpy as jnp
from jax import lax
from jax.experimental import pallas as pl
from jax.experimental.pallas import tpu as pltpu
from jax.sharding import PartitionSpec as P

MESH = pl.DeviceIdType.MESH
F32 = jnp.float32
BF16 = jnp.bfloat16
FEAT = 64
RHS = 16
PTS = 64
NX = 4
LOG2E = math.log2(math.e)
SCALE = math.sqrt(5.0) * LOG2E
TINY = 1e-30


def half_lanes(shape):
    return lax.broadcasted_iota(jnp.int32, shape, 1) < 64


def swap(x):
    return pltpu.roll(x, 64, 1)


def split3(s):
    a = s.astype(BF16).astype(F32)
    b = (s - a).astype(BF16).astype(F32)
    c = (s - a - b).astype(BF16).astype(F32)
    return a, b, c


def kernel(
    nrow, ncol,
    points_hbm, scale_hbm, noise_hbm, residual_hbm, direction_hbm,
    image_out, alpha_out, beta_out,
    points, scale, noise, residual, direction,
    cbuf, rbuf, rmat, amat, kbuf, prod, psend, pbuf, stat_a, stat_b, tot_a, tot_b,
    in_sem, c_send, z_recv, x_recv, r_send, y_recv, k_recv,
    p_send, p_recv, a_send, a_recv, b_send, b_recv,
):
    nz, ny = ncol // NX, nrow // 2
    row, col = lax.axis_index("row"), lax.axis_index("col")
    x, z, y, k = col // nz, col % nz, row // 2, row % 2

    def device(dx=0, dy=0, dz=0, dk=0):
        return (
            lax.rem(y + dy, ny) * 2 + lax.rem(k + dk, 2),
            lax.rem(x + dx, NX) * nz + lax.rem(z + dz, nz),
        )

    def near_first(n):
        steps = []
        for s in range(1, n // 2 + 1):
            steps += [s] if 2 * s == n else [s, n - s]
        return steps

    zs, ys, xs = near_first(nz), near_first(ny), near_first(NX)
    far_zs, far_ys, far_xs = zs[::-1], ys[::-1], xs[::-1]
    row_steps = [(dy, dk) for dy in far_ys + [0] for dk in (1, 0) if (dy, dk) != (0, 0)]
    col_steps = [(dz, dx) for dz in far_zs + [0] for dx in far_xs + [0] if (dz, dx) != (0, 0)]

    loads = []
    for i, (src, dst) in enumerate((
            (points_hbm, points), (scale_hbm, scale), (direction_hbm, direction),
            (noise_hbm, noise), (residual_hbm, residual))):
        copy = pltpu.make_async_copy(src, dst, in_sem.at[i])
        copy.start()
        loads.append(copy)

    barrier = pltpu.get_barrier_semaphore()
    greeted = (
        [device(dz=s) for s in far_zs] + [device(dy=s) for s in far_ys]
        + [device(dx=s) for s in far_xs] + [device(dk=1)])
    for peer in greeted:
        pl.semaphore_signal(barrier, inc=1, device_id=peer, device_id_type=MESH)

    for copy in loads[:3]:
        copy.wait()
    ls_col = jnp.transpose(jnp.broadcast_to(scale[...], (FEAT, FEAT)))
    zf = points[...] / ls_col * SCALE
    hi = zf.astype(BF16).astype(F32)
    lo = (zf - hi).astype(BF16).astype(F32)
    rbuf[0, 0] = jnp.concatenate([hi, lo], axis=1).astype(BF16)
    sq = jnp.sum((hi + lo) * (hi + lo), axis=0, keepdims=True)
    s1, s2, s3 = split3(sq)
    one = jnp.ones_like(sq)
    ext = jnp.concatenate([s1, s2, s3, one, one, one, one * 0, one * 0], axis=0)
    pad = jnp.zeros((FEAT - 8, PTS), F32)
    hi_t = jnp.transpose(hi)
    lo_t = jnp.transpose(lo)
    ext_t = jnp.transpose(jnp.concatenate([ext, pad], axis=0))
    cbuf[0, 0, 0:64, :] = jnp.concatenate([hi_t, lo_t], axis=1).astype(BF16)
    own_dir = direction[...]
    packed = jnp.concatenate([own_dir, ext_t[0:16]], axis=1)
    lane16 = lax.broadcasted_iota(jnp.int32, (16, 128), 1)
    for a in range(1, 4):
        piece = jnp.concatenate([ext_t[16 * a:16 * a + 16], jnp.zeros((16, 64), F32)], axis=1)
        packed = jnp.where((lane16 >= 64 + 8 * a) & (lane16 < 72 + 8 * a), pltpu.roll(piece, 64 + 8 * a, 1), packed)
    cbuf[0, 0, 64:80, :] = packed.astype(BF16)

    pl.semaphore_wait(barrier, len(greeted))

    sends = []

    def send(src, dst, ssem, rsem, peer):
        copy = pltpu.make_async_remote_copy(
            src_ref=src, dst_ref=dst, send_sem=ssem, recv_sem=rsem,
            device_id=peer, device_id_type=MESH)
        copy.start()
        sends.append(copy)

    def arrived(ref, sem):
        pltpu.make_async_copy(ref, ref, sem).wait()

    def to_x(dz):
        for dx in far_xs:
            send(cbuf.at[dz, 0], cbuf.at[dz, dx], c_send.at[dz, dx], x_recv.at[dz], device(dx=dx))

    def to_core(dy):
        send(rbuf.at[dy, 0], rbuf.at[dy, 1], r_send.at[dy, 1], k_recv.at[dy], device(dk=1))

    for dz, dy in zip(far_zs, far_ys):
        send(cbuf.at[0, 0], cbuf.at[dz, 0], c_send.at[dz, 0], z_recv.at[dz], device(dz=dz))
        send(rbuf.at[0, 0], rbuf.at[dy, 0], r_send.at[dy, 0], y_recv.at[dy], device(dy=dy))
    to_x(0)
    to_core(0)
    for dz, dy in zip(zs, ys):
        arrived(cbuf.at[dz, 0], z_recv.at[dz])
        to_x(dz)
        arrived(rbuf.at[dy, 0], y_recv.at[dy])
        to_core(dy)

    left = half_lanes((FEAT, 128))
    sub = lax.broadcasted_iota(jnp.int32, (64, 128), 0)
    for dy in [0] + ys:
        arrived(rbuf.at[dy, 1], k_recv.at[dy])
        c0 = rbuf[dy, 0].astype(F32)
        c1 = rbuf[dy, 1].astype(F32)
        h = jnp.where(left, c0, swap(c1))
        l = jnp.where(left, swap(c0), c1)
        t1, t2, t3 = split3(jnp.sum((h + l) * (h + l), axis=0, keepdims=True))
        e = jnp.where(sub < 3, 1.0, jnp.where(sub == 3, t1, jnp.where(sub == 4, t2, jnp.where(sub == 5, t3, 0.0))))
        lanes = slice(128 * dy, 128 * dy + 128)
        h2 = (-2.0 * h).astype(BF16)
        rmat[0:64, lanes] = h2
        rmat[64:128, lanes] = h2
        rmat[128:192, lanes] = (-2.0 * l).astype(BF16)
        rmat[192:256, lanes] = e.astype(BF16)

    left16 = half_lanes((16, 128))
    width = 256
    blocks = [slice(width * i, width * i + width) for i in range(nrow * PTS // width)]

    def operands(dz):
        dirs = []
        for dx in range(NX):
            tail = cbuf[dz, dx, 64:80, :].astype(F32)
            dirs.append(tail)
            for a in range(4):
                rows = slice(64 * dx + 16 * a, 64 * dx + 16 * a + 16)
                body = cbuf[dz, dx, 16 * a:16 * a + 16, :]
                amat[rows, 0:128] = body
                shifted = tail if a == 0 else pltpu.roll(tail, 128 - 8 * a, 1)
                amat[rows, 128:256] = jnp.where(left16, body.astype(F32), shifted).astype(BF16)
        return jnp.concatenate(
            [jnp.where(left16, dirs[0], swap(dirs[1])), jnp.where(left16, dirs[2], swap(dirs[3]))], axis=1).astype(BF16)

    def entries(lanes):
        dist = jnp.dot(amat[...], rmat[:, lanes], preferred_element_type=F32)
        dist = jnp.maximum(dist, TINY)
        v = dist * lax.rsqrt(dist)
        w = v * (1.0 / (LOG2E * math.sqrt(3.0))) + math.sqrt(0.75)
        return ((w * w + 0.25) * jnp.exp2(-v)).astype(BF16)

    before = None
    for n, dz in enumerate([0] + zs):
        arrived(cbuf.at[dz, pl.ds(1, NX - 1)], x_recv.at[dz])
        dgrp = operands(dz)
        for lanes in blocks:
            kern = entries(lanes)
            if n == 1:
                prod[:, lanes] = jnp.dot(before, kbuf[(n - 1) % 2, :, lanes], preferred_element_type=F32)
            elif n > 1:
                prod[:, lanes] += jnp.dot(before, kbuf[(n - 1) % 2, :, lanes], preferred_element_type=F32)
            kbuf[n % 2, :, lanes] = kern
        before = dgrp
    for lanes in blocks:
        prod[:, lanes] += jnp.dot(before, kbuf[(nz - 1) % 2, :, lanes], preferred_element_type=F32)

    left8 = half_lanes((8, 128))
    for dy in far_ys + [0]:
        top = prod[0:8, 128 * dy:128 * dy + 128]
        bottom = prod[8:16, 128 * dy:128 * dy + 128]
        psend[dy, 0] = jnp.where(left8, top, swap(bottom))
        psend[dy, 1] = jnp.where(left8, swap(top), bottom)
    for dy, dk in row_steps:
        send(psend.at[dy, dk], pbuf.at[dy * 2 + dk], p_send.at[dy, dk], p_recv, device(dy=ny - dy, dk=dk))
    pbuf[0] = psend[0, 0]
    loads[3].wait()
    loads[4].wait()
    res = residual[...]
    arrived(pbuf.at[pl.ds(1, nrow - 1)], p_recv)
    total = jnp.sum(pbuf[...], axis=0)
    image = jnp.concatenate([total, swap(total)], axis=0)[:, 0:64] + noise[...] * own_dir
    image_out[...] = image

    def norm(a, b):
        return jnp.sum(a * b, axis=1, keepdims=True)

    stats = jnp.where(
        lane16 == 0, norm(res, res),
        jnp.where(lane16 == 1, norm(own_dir, image),
                  jnp.where(lane16 == 2, norm(res, image),
                            jnp.where(lane16 == 3, norm(image, image), 0.0))))
    tot_a[...] = stats[0:8] + swap(stats[8:16])
    for dy, dk in row_steps:
        send(tot_a, stat_a.at[dy * 2 + dk], a_send.at[dy, dk], a_recv, device(dy=dy, dk=dk))
    stat_a[0] = tot_a[...]
    arrived(stat_a.at[pl.ds(1, nrow - 1)], a_recv)
    tot_b[...] = jnp.sum(stat_a[...], axis=0)
    for dz, dx in col_steps:
        send(tot_b, stat_b.at[dz * NX + dx], b_send.at[dz, dx], b_recv, device(dz=dz, dx=dx))
    stat_b[0] = tot_b[...]
    arrived(stat_b.at[pl.ds(1, ncol - 1)], b_recv)
    total = jnp.sum(stat_b[...], axis=0)
    total = jnp.concatenate([total, swap(total)], axis=0)
    rr, curv, cross, square = (total[:, i:i + 1] for i in range(4))
    alpha = rr / curv
    rr_new = jnp.maximum(rr - 2.0 * (alpha * cross) + alpha * (alpha * square), 0.0)
    beta = rr_new / rr
    alpha_out[...] = jnp.broadcast_to(alpha, (RHS, PTS))
    beta_out[...] = jnp.broadcast_to(beta, (RHS, PTS))
    for copy in sends:
        copy.wait_send()


def solution(mesh):
    nrow, ncol = mesh.shape["row"], mesh.shape["col"]
    nz, ny = ncol // NX, nrow // 2
    spread = P(None, ("row", "col"))
    placed = (spread, P(), P(("row", "col")), spread, spread, spread)
    vmem = pl.BlockSpec(memory_space=pltpu.VMEM)
    dma = pltpu.SemaphoreType.DMA
    shape = jax.ShapeDtypeStruct((RHS, PTS), F32)

    step = pl.pallas_call(
        functools.partial(kernel, nrow, ncol),
        out_shape=(shape, shape, shape),
        in_specs=[pl.BlockSpec(memory_space=pltpu.HBM)] * 5,
        out_specs=(vmem,) * 3,
        scratch_shapes=[
            pltpu.VMEM((FEAT, PTS), F32),
            pltpu.VMEM((1, FEAT), F32),
            pltpu.VMEM((1, PTS), F32),
            pltpu.VMEM((RHS, PTS), F32),
            pltpu.VMEM((RHS, PTS), F32),
            pltpu.VMEM((nz, NX, 80, 128), BF16),
            pltpu.VMEM((ny, 2, 64, 128), BF16),
            pltpu.VMEM((256, nrow * PTS), BF16),
            pltpu.VMEM((256, 256), BF16),
            pltpu.VMEM((2, 256, nrow * PTS), BF16),
            pltpu.VMEM((RHS, nrow * PTS), F32),
            pltpu.VMEM((ny, 2, 8, 128), F32),
            pltpu.VMEM((nrow, 8, 128), F32),
            pltpu.VMEM((nrow, 8, 128), F32),
            pltpu.VMEM((ncol, 8, 128), F32),
            pltpu.VMEM((8, 128), F32),
            pltpu.VMEM((8, 128), F32),
            dma((5,)), dma((nz, NX)), dma((nz,)), dma((nz,)), dma((ny, 2)), dma((ny,)), dma((ny,)),
            dma((ny, 2)), dma, dma((ny, 2)), dma, dma((nz, NX)), dma,
        ],
        compiler_params=pltpu.CompilerParams(
            collective_id=0, has_side_effects=True, vmem_limit_bytes=60 * 1024 * 1024),
        name="cg_step",
    )

    def on_device(points, lengthscale, noise, iterate, residual, direction):
        image, alpha, beta = step(
            points, lengthscale.reshape(1, FEAT), noise.reshape(1, PTS), residual, direction)
        fresh = residual - alpha * image
        return iterate + alpha * direction, fresh, fresh + beta * direction

    return jax.shard_map(
        on_device, mesh=mesh, in_specs=placed, out_specs=(spread, spread, spread), check_vma=False)
```

```python
import functools
import math

import jax
import jax.numpy as jnp
from jax import lax
from jax.experimental import pallas as pl
from jax.experimental.pallas import tpu as pltpu
from jax.sharding import PartitionSpec as P

MESH = pl.DeviceIdType.MESH
F32 = jnp.float32
BF16 = jnp.bfloat16
FEAT = 64
RHS = 16
PTS = 64
NX = 4
LOG2E = math.log2(math.e)
SCALE = math.sqrt(5.0)
TINY = 1e-30
Z_MAX = 3.0
STEEP = 251.0 / Z_MAX
LOW = 125.0


def half_lanes(shape):
    return lax.broadcasted_iota(jnp.int32, shape, 1) < 64


def swap(x):
    return pltpu.roll(x, 64, 1)


def split3(s):
    a = s.astype(BF16).astype(F32)
    b = (s - a).astype(BF16).astype(F32)
    c = (s - a - b).astype(BF16).astype(F32)
    return a, b, c


def encode(z):
    mag = jnp.exp2(jnp.abs(z) * STEEP - LOW)
    return jnp.where(z < 0, -mag, mag).astype(BF16)


def decode(code):
    w = code.astype(F32)
    z = (jnp.log2(jnp.abs(w)) + LOW) * (SCALE / STEEP)
    return jnp.where(w < 0, -z, z)


def kernel(
    nrow, ncol,
    points_hbm, scale_hbm, noise_hbm, residual_hbm, direction_hbm,
    image_out, alpha_out, beta_out,
    points, scale, noise, residual, direction,
    cbuf, rbuf, rmat, amat, kbuf, prod, psend, pbuf, stat_a, stat_b, tot_a, tot_b,
    in_sem, c_send, z_recv, x_recv, r_send, y_recv, k_recv,
    p_send, p_recv, a_send, a_recv, b_send, b_recv,
):
    nz, ny = ncol // NX, nrow // 2
    row, col = lax.axis_index("row"), lax.axis_index("col")
    x, z, y, k = col // nz, col % nz, row // 2, row % 2

    def device(dx=0, dy=0, dz=0, dk=0):
        return (
            lax.rem(y + dy, ny) * 2 + lax.rem(k + dk, 2),
            lax.rem(x + dx, NX) * nz + lax.rem(z + dz, nz),
        )

    def near_first(n):
        steps = []
        for s in range(1, n // 2 + 1):
            steps += [s] if 2 * s == n else [s, n - s]
        return steps

    zs, ys, xs = near_first(nz), near_first(ny), near_first(NX)
    far_zs, far_ys, far_xs = zs[::-1], ys[::-1], xs[::-1]
    row_steps = [(dy, dk) for dy in far_ys + [0] for dk in (1, 0) if (dy, dk) != (0, 0)]
    col_steps = [(dz, dx) for dz in far_zs + [0] for dx in far_xs + [0] if (dz, dx) != (0, 0)]

    barrier = pltpu.get_barrier_semaphore()
    greeted = (
        [device(dz=s) for s in far_zs] + [device(dy=s) for s in far_ys]
        + [device(dx=s) for s in far_xs] + [device(dk=1)])
    for peer in greeted:
        pl.semaphore_signal(barrier, inc=1, device_id=peer, device_id_type=MESH)

    loads = []
    for i, (src, dst) in enumerate((
            (points_hbm, points), (scale_hbm, scale), (direction_hbm, direction),
            (noise_hbm, noise), (residual_hbm, residual))):
        copy = pltpu.make_async_copy(src, dst, in_sem.at[i])
        copy.start()
        loads.append(copy)

    for copy in loads[:3]:
        copy.wait()
    ls_col = jnp.transpose(jnp.broadcast_to(scale[...], (FEAT, FEAT)))
    code = encode(points[...] / ls_col)
    zf = decode(code)
    hi = zf.astype(BF16).astype(F32)
    lo = (zf - hi).astype(BF16).astype(F32)
    code = code.astype(F32)
    half = FEAT // 2
    rbuf[0, 0] = jnp.concatenate([code[0:half], code[half:FEAT]], axis=1).astype(BF16)
    sq = jnp.sum((hi + lo) * (hi + lo), axis=0, keepdims=True)
    s1, s2, s3 = split3(sq)
    one = jnp.ones_like(sq)
    ext = jnp.concatenate([s1, s2, s3, one, one, one, one * 0, one * 0], axis=0)
    pad = jnp.zeros((FEAT - 8, PTS), F32)
    code_t = jnp.transpose(code)
    ext_t = jnp.transpose(jnp.concatenate([ext, pad], axis=0))
    cbuf[0, 0, 0:32, :] = jnp.concatenate([code_t[0:32], code_t[32:64]], axis=1).astype(BF16)
    own_dir = direction[...]
    packed = jnp.concatenate([own_dir, ext_t[0:16]], axis=1)
    lane16 = lax.broadcasted_iota(jnp.int32, (16, 128), 1)
    for a in range(1, 4):
        piece = jnp.concatenate([ext_t[16 * a:16 * a + 16], jnp.zeros((16, 64), F32)], axis=1)
        packed = jnp.where((lane16 >= 64 + 8 * a) & (lane16 < 72 + 8 * a), pltpu.roll(piece, 64 + 8 * a, 1), packed)
    cbuf[0, 0, 32:48, :] = packed.astype(BF16)

    pl.semaphore_wait(barrier, len(greeted))

    sends = []

    def send(src, dst, ssem, rsem, peer):
        copy = pltpu.make_async_remote_copy(
            src_ref=src, dst_ref=dst, send_sem=ssem, recv_sem=rsem,
            device_id=peer, device_id_type=MESH)
        copy.start()
        sends.append(copy)

    def arrived(ref, sem):
        pltpu.make_async_copy(ref, ref, sem).wait()

    def to_x(dz):
        for dx in far_xs:
            send(cbuf.at[dz, 0], cbuf.at[dz, dx], c_send.at[dz, dx], x_recv.at[dz], device(dx=dx))

    def to_core(dy):
        send(rbuf.at[dy, 0], rbuf.at[dy, 1], r_send.at[dy, 1], k_recv.at[dy], device(dk=1))

    for dz, dy in zip(far_zs, far_ys):
        send(cbuf.at[0, 0], cbuf.at[dz, 0], c_send.at[dz, 0], z_recv.at[dz], device(dz=dz))
        send(rbuf.at[0, 0], rbuf.at[dy, 0], r_send.at[dy, 0], y_recv.at[dy], device(dy=dy))
    to_x(0)
    to_core(0)
    def forward(dz, dy):
        arrived(cbuf.at[dz, 0], z_recv.at[dz])
        to_x(dz)
        arrived(rbuf.at[dy, 0], y_recv.at[dy])
        to_core(dy)

    near_ys = [0] + ys
    left = half_lanes((FEAT // 2, 128))
    sub = lax.broadcasted_iota(jnp.int32, (64, 128), 0)

    def row_operand(n):
        dy = near_ys[n]
        arrived(rbuf.at[dy, 1], k_recv.at[dy])
        c0 = decode(rbuf[dy, 0])
        c1 = decode(rbuf[dy, 1])
        full = jnp.concatenate([jnp.where(left, c0, swap(c1)), jnp.where(left, swap(c0), c1)], axis=0)
        h = full.astype(BF16).astype(F32)
        l = (full - h).astype(BF16).astype(F32)
        t1, t2, t3 = split3(jnp.sum((h + l) * (h + l), axis=0, keepdims=True))
        e = jnp.where(sub < 3, 1.0, jnp.where(sub == 3, t1, jnp.where(sub == 4, t2, jnp.where(sub == 5, t3, 0.0))))
        lanes = slice(128 * n, 128 * n + 128)
        h2 = (-2.0 * h).astype(BF16)
        rmat[0:64, lanes] = h2
        rmat[64:128, lanes] = h2
        rmat[128:192, lanes] = (-2.0 * l).astype(BF16)
        rmat[192:256, lanes] = e.astype(BF16)

    left16 = half_lanes((16, 128))
    width = 256
    blocks = [slice(width * i, width * i + width) for i in range(nrow * PTS // width)]
    dirs_of = {}

    def col_operand(dz):
        arrived(cbuf.at[dz, pl.ds(1, NX - 1)], x_recv.at[dz])
        dirs = []
        for dx in range(NX):
            tail = cbuf[dz, dx, 32:48, :].astype(F32)
            dirs.append(tail)
            full = decode(cbuf[dz, dx, 0:32, :])
            high = full.astype(BF16).astype(F32)
            low = full - high
            for a in range(4):
                rows = slice(64 * dx + 16 * a, 64 * dx + 16 * a + 16)
                part = slice(16 * (a % 2), 16 * (a % 2) + 16)
                h, l = high[part], low[part]
                h, l = (h, swap(l)) if a < 2 else (swap(h), l)
                extra = tail if a == 0 else pltpu.roll(tail, 128 - 8 * a, 1)
                amat[dz, rows, 0:128] = jnp.where(left16, h, l).astype(BF16)
                amat[dz, rows, 128:256] = jnp.where(left16, h, extra).astype(BF16)
        dirs_of[dz] = jnp.concatenate(
            [jnp.where(left16, dirs[0], swap(dirs[1])), jnp.where(left16, dirs[2], swap(dirs[3]))], axis=1).astype(BF16)

    pending = []
    begun = set()

    def product():
        dz, i = pending.pop()
        part = jnp.dot(dirs_of[dz], kbuf[dz, :, blocks[i]], preferred_element_type=F32)
        prod[:, blocks[i]] = prod[:, blocks[i]] + part if i in begun else part
        begun.add(i)

    def entries(dz, i):
        dist = jnp.dot(amat[dz], rmat[:, blocks[i]], preferred_element_type=F32)
        dist = jnp.maximum(dist, TINY)
        root = dist * lax.rsqrt(dist)
        kern = ((dist * (1.0 / 3.0) + 1.0 + root) * jnp.exp2(root * -LOG2E)).astype(BF16)
        if pending:
            product()
        kbuf[dz, :, blocks[i]] = kern
        pending.append((dz, i))

    left8 = half_lanes((8, 128))

    def scatter(i):
        for n in (2 * i + 1, 2 * i):
            dy = near_ys[n]
            top = prod[0:8, 128 * n:128 * n + 128]
            bottom = prod[8:16, 128 * n:128 * n + 128]
            psend[dy, 0] = jnp.where(left8, top, swap(bottom))
            psend[dy, 1] = jnp.where(left8, swap(top), bottom)
            for dk in (1, 0):
                if (dy, dk) != (0, 0):
                    send(psend.at[dy, dk], pbuf.at[dy * 2 + dk], p_send.at[dy, dk], p_recv, device(dy=ny - dy, dk=dk))

    for dz, dy in zip(zs, ys):
        forward(dz, dy)
    for n in range(8):
        row_operand(n)
    for dz in [0] + zs[:-1]:
        col_operand(dz)
        for i in range(4):
            entries(dz, i)
    col_operand(zs[-1])
    for i in (3, 2, 1, 0):
        entries(zs[-1], i)
        if i < 3:
            scatter(i + 1)
    product()
    scatter(0)

    pbuf[0] = psend[0, 0]
    loads[3].wait()
    loads[4].wait()
    res = residual[...]
    arrived(pbuf.at[pl.ds(1, nrow - 1)], p_recv)
    total = jnp.sum(pbuf[...], axis=0)
    image = jnp.concatenate([total, swap(total)], axis=0)[:, 0:64] + noise[...] * own_dir
    image_out[...] = image

    def norm(a, b):
        return jnp.sum(a * b, axis=1, keepdims=True)

    stats = jnp.where(
        lane16 == 0, norm(res, res),
        jnp.where(lane16 == 1, norm(own_dir, image),
                  jnp.where(lane16 == 2, norm(res, image),
                            jnp.where(lane16 == 3, norm(image, image), 0.0))))
    tot_a[...] = stats[0:8] + swap(stats[8:16])
    for dy, dk in row_steps:
        send(tot_a, stat_a.at[dy * 2 + dk], a_send.at[dy, dk], a_recv, device(dy=dy, dk=dk))
    stat_a[0] = tot_a[...]
    arrived(stat_a.at[pl.ds(1, nrow - 1)], a_recv)
    tot_b[...] = jnp.sum(stat_a[...], axis=0)
    for dz, dx in col_steps:
        send(tot_b, stat_b.at[dz * NX + dx], b_send.at[dz, dx], b_recv, device(dz=dz, dx=dx))
    stat_b[0] = tot_b[...]
    arrived(stat_b.at[pl.ds(1, ncol - 1)], b_recv)
    total = jnp.sum(stat_b[...], axis=0)
    total = jnp.concatenate([total, swap(total)], axis=0)
    rr, curv, cross, square = (total[:, i:i + 1] for i in range(4))
    alpha = rr / curv
    rr_new = jnp.maximum(rr - 2.0 * (alpha * cross) + alpha * (alpha * square), 0.0)
    beta = rr_new / rr
    alpha_out[...] = jnp.broadcast_to(alpha, (RHS, PTS))
    beta_out[...] = jnp.broadcast_to(beta, (RHS, PTS))
    for copy in sends:
        copy.wait_send()


def solution(mesh):
    nrow, ncol = mesh.shape["row"], mesh.shape["col"]
    nz, ny = ncol // NX, nrow // 2
    spread = P(None, ("row", "col"))
    placed = (spread, P(), P(("row", "col")), spread, spread, spread)
    vmem = pl.BlockSpec(memory_space=pltpu.VMEM)
    dma = pltpu.SemaphoreType.DMA
    shape = jax.ShapeDtypeStruct((RHS, PTS), F32)

    step = pl.pallas_call(
        functools.partial(kernel, nrow, ncol),
        out_shape=(shape, shape, shape),
        in_specs=[pl.BlockSpec(memory_space=pltpu.HBM)] * 5,
        out_specs=(vmem,) * 3,
        scratch_shapes=[
            pltpu.VMEM((FEAT, PTS), F32),
            pltpu.VMEM((1, FEAT), F32),
            pltpu.VMEM((1, PTS), F32),
            pltpu.VMEM((RHS, PTS), F32),
            pltpu.VMEM((RHS, PTS), F32),
            pltpu.VMEM((nz, NX, 48, 128), BF16),
            pltpu.VMEM((ny, 2, 32, 128), BF16),
            pltpu.VMEM((256, nrow * PTS), BF16),
            pltpu.VMEM((nz, 256, 256), BF16),
            pltpu.VMEM((nz, 256, nrow * PTS), BF16),
            pltpu.VMEM((RHS, nrow * PTS), F32),
            pltpu.VMEM((ny, 2, 8, 128), F32),
            pltpu.VMEM((nrow, 8, 128), F32),
            pltpu.VMEM((nrow, 8, 128), F32),
            pltpu.VMEM((ncol, 8, 128), F32),
            pltpu.VMEM((8, 128), F32),
            pltpu.VMEM((8, 128), F32),
            dma((5,)), dma((nz, NX)), dma((nz,)), dma((nz,)), dma((ny, 2)), dma((ny,)), dma((ny,)),
            dma((ny, 2)), dma, dma((ny, 2)), dma, dma((nz, NX)), dma,
        ],
        compiler_params=pltpu.CompilerParams(
            collective_id=0, has_side_effects=True, vmem_limit_bytes=539 * 1024 * 1024 // 10),
        name="cg_step",
    )

    def on_device(points, lengthscale, noise, iterate, residual, direction):
        image, alpha, beta = step(
            points, lengthscale.reshape(1, FEAT), noise.reshape(1, PTS), residual, direction)
        fresh = residual - alpha * image
        return iterate + alpha * direction, fresh, fresh + beta * direction

    return jax.shard_map(
        on_device, mesh=mesh, in_specs=placed, out_specs=(spread, spread, spread), check_vma=False)
```

```python
import functools
import math

import jax
import jax.numpy as jnp
from jax import lax
from jax.experimental import pallas as pl
from jax.experimental.pallas import tpu as pltpu
from jax.sharding import PartitionSpec as P

MESH = pl.DeviceIdType.MESH
F32 = jnp.float32
BF16 = jnp.bfloat16
FEAT = 64
RHS = 16
PTS = 64
NX = 4
LOG2E = math.log2(math.e)
SCALE = math.sqrt(5.0)
TINY = 1e-30
Z_MAX = 3.0
STEEP = 251.0 / Z_MAX
LOW = 125.0


def half_lanes(shape):
    return lax.broadcasted_iota(jnp.int32, shape, 1) < 64


def swap(x):
    return pltpu.roll(x, 64, 1)


def split3(s):
    a = s.astype(BF16).astype(F32)
    b = (s - a).astype(BF16).astype(F32)
    c = (s - a - b).astype(BF16).astype(F32)
    return a, b, c


def encode(z):
    mag = jnp.exp2(jnp.abs(z) * STEEP - LOW)
    return jnp.where(z < 0, -mag, mag).astype(BF16)


def decode(code):
    w = code.astype(F32)
    z = (jnp.log2(jnp.abs(w)) + LOW) * (SCALE / STEEP)
    return jnp.where(w < 0, -z, z)


def kernel(
    nrow, ncol,
    points_hbm, scale_hbm, noise_hbm, residual_hbm, direction_hbm,
    image_out, alpha_out, beta_out,
    points, scale, noise, residual, direction,
    cbuf, rbuf, rmat, amat, kbuf, prod, psend, pbuf, stat_a, stat_b, tot_a, tot_b,
    in_sem, c_send, z_recv, x_recv, r_send, y_recv, k_recv,
    p_send, p_recv, a_send, a_recv, b_send, b_recv,
):
    nz, ny = ncol // NX, nrow // 2
    row, col = lax.axis_index("row"), lax.axis_index("col")
    x, z, y, k = col // nz, col % nz, row // 2, row % 2

    def device(dx=0, dy=0, dz=0, dk=0):
        return (
            lax.rem(y + dy, ny) * 2 + lax.rem(k + dk, 2),
            lax.rem(x + dx, NX) * nz + lax.rem(z + dz, nz),
        )

    def near_first(n):
        steps = []
        for s in range(1, n // 2 + 1):
            steps += [s] if 2 * s == n else [s, n - s]
        return steps

    zs, ys, xs = near_first(nz), near_first(ny), near_first(NX)
    far_zs, far_ys, far_xs = zs[::-1], ys[::-1], xs[::-1]
    row_steps = [(dy, dk) for dy in far_ys + [0] for dk in (1, 0) if (dy, dk) != (0, 0)]
    col_steps = [(dz, dx) for dz in far_zs + [0] for dx in far_xs + [0] if (dz, dx) != (0, 0)]

    barrier = pltpu.get_barrier_semaphore()
    greeted = (
        [device(dz=s) for s in far_zs] + [device(dy=s) for s in far_ys]
        + [device(dx=s) for s in far_xs] + [device(dk=1)])
    for peer in greeted:
        pl.semaphore_signal(barrier, inc=1, device_id=peer, device_id_type=MESH)

    loads = []
    for i, (src, dst) in enumerate((
            (points_hbm, points), (scale_hbm, scale), (direction_hbm, direction),
            (noise_hbm, noise), (residual_hbm, residual))):
        copy = pltpu.make_async_copy(src, dst, in_sem.at[i])
        copy.start()
        loads.append(copy)

    for copy in loads[:3]:
        copy.wait()
    ls_col = jnp.transpose(jnp.broadcast_to(scale[...], (FEAT, FEAT)))
    code = encode(points[...] / ls_col)
    zf = decode(code)
    hi = zf.astype(BF16).astype(F32)
    lo = (zf - hi).astype(BF16).astype(F32)
    code = code.astype(F32)
    half = FEAT // 2
    rbuf[0, 0] = jnp.concatenate([code[0:half], code[half:FEAT]], axis=1).astype(BF16)
    sq = jnp.sum((hi + lo) * (hi + lo), axis=0, keepdims=True)
    s1, s2, s3 = split3(sq)
    one = jnp.ones_like(sq)
    ext = jnp.concatenate([s1, s2, s3, one, one, one, one * 0, one * 0], axis=0)
    pad = jnp.zeros((FEAT - 8, PTS), F32)
    code_t = jnp.transpose(code)
    ext_t = jnp.transpose(jnp.concatenate([ext, pad], axis=0))
    cbuf[0, 0, 0:32, :] = jnp.concatenate([code_t[0:32], code_t[32:64]], axis=1).astype(BF16)
    own_dir = direction[...]
    packed = jnp.concatenate([own_dir, ext_t[0:16]], axis=1)
    lane16 = lax.broadcasted_iota(jnp.int32, (16, 128), 1)
    for a in range(1, 4):
        piece = jnp.concatenate([ext_t[16 * a:16 * a + 16], jnp.zeros((16, 64), F32)], axis=1)
        packed = jnp.where((lane16 >= 64 + 8 * a) & (lane16 < 72 + 8 * a), pltpu.roll(piece, 64 + 8 * a, 1), packed)
    cbuf[0, 0, 32:48, :] = packed.astype(BF16)

    pl.semaphore_wait(barrier, len(greeted))

    sends = []

    def send(src, dst, ssem, rsem, peer):
        copy = pltpu.make_async_remote_copy(
            src_ref=src, dst_ref=dst, send_sem=ssem, recv_sem=rsem,
            device_id=peer, device_id_type=MESH)
        copy.start()
        sends.append(copy)

    def arrived(ref, sem):
        pltpu.make_async_copy(ref, ref, sem).wait()

    def to_x(dz):
        for dx in far_xs:
            send(cbuf.at[dz, 0], cbuf.at[dz, dx], c_send.at[dz, dx], x_recv.at[dz], device(dx=dx))

    def to_core(dy):
        send(rbuf.at[dy, 0], rbuf.at[dy, 1], r_send.at[dy, 1], k_recv.at[dy], device(dk=1))

    for dz, dy in zip(far_zs, far_ys):
        send(cbuf.at[0, 0], cbuf.at[dz, 0], c_send.at[dz, 0], z_recv.at[dz], device(dz=dz))
        send(rbuf.at[0, 0], rbuf.at[dy, 0], r_send.at[dy, 0], y_recv.at[dy], device(dy=dy))
    to_x(0)
    to_core(0)
    def forward(dz, dy):
        arrived(cbuf.at[dz, 0], z_recv.at[dz])
        to_x(dz)
        arrived(rbuf.at[dy, 0], y_recv.at[dy])
        to_core(dy)

    near_ys = [0] + ys
    left = half_lanes((FEAT // 2, 128))
    sub = lax.broadcasted_iota(jnp.int32, (64, 128), 0)

    def row_operand(n):
        dy = near_ys[n]
        arrived(rbuf.at[dy, 1], k_recv.at[dy])
        c0 = decode(rbuf[dy, 0])
        c1 = decode(rbuf[dy, 1])
        full = jnp.concatenate([jnp.where(left, c0, swap(c1)), jnp.where(left, swap(c0), c1)], axis=0)
        h = full.astype(BF16).astype(F32)
        l = (full - h).astype(BF16).astype(F32)
        t1, t2, t3 = split3(jnp.sum((h + l) * (h + l), axis=0, keepdims=True))
        e = jnp.where(sub < 3, 1.0, jnp.where(sub == 3, t1, jnp.where(sub == 4, t2, jnp.where(sub == 5, t3, 0.0))))
        lanes = slice(128 * n, 128 * n + 128)
        h2 = (-2.0 * h).astype(BF16)
        rmat[0:64, lanes] = h2
        rmat[64:128, lanes] = h2
        rmat[128:192, lanes] = (-2.0 * l).astype(BF16)
        rmat[192:256, lanes] = e.astype(BF16)

    left16 = half_lanes((16, 128))
    width = 256
    blocks = [slice(width * i, width * i + width) for i in range(nrow * PTS // width)]
    dirs_of = {}

    def col_operand(dz):
        arrived(cbuf.at[dz, pl.ds(1, NX - 1)], x_recv.at[dz])
        dirs = []
        for dx in range(NX):
            tail = cbuf[dz, dx, 32:48, :].astype(F32)
            dirs.append(tail)
            full = decode(cbuf[dz, dx, 0:32, :])
            high = full.astype(BF16).astype(F32)
            low = full - high
            for a in range(4):
                rows = slice(64 * dx + 16 * a, 64 * dx + 16 * a + 16)
                part = slice(16 * (a % 2), 16 * (a % 2) + 16)
                h, l = high[part], low[part]
                h, l = (h, swap(l)) if a < 2 else (swap(h), l)
                extra = tail if a == 0 else pltpu.roll(tail, 128 - 8 * a, 1)
                amat[dz, rows, 0:128] = jnp.where(left16, h, l).astype(BF16)
                amat[dz, rows, 128:256] = jnp.where(left16, h, extra).astype(BF16)
        dirs_of[dz] = jnp.concatenate(
            [jnp.where(left16, dirs[0], swap(dirs[1])), jnp.where(left16, dirs[2], swap(dirs[3]))], axis=1).astype(BF16)

    pending = []
    begun = set()

    def product():
        dz, i = pending.pop()
        part = jnp.dot(dirs_of[dz], kbuf[dz, :, blocks[i]], preferred_element_type=F32)
        prod[:, blocks[i]] = prod[:, blocks[i]] + part if i in begun else part
        begun.add(i)

    def entries(dz, i):
        dist = jnp.dot(amat[dz], rmat[:, blocks[i]], preferred_element_type=F32)
        dist = jnp.maximum(dist, TINY)
        root = dist * lax.rsqrt(dist)
        kern = ((dist * (1.0 / 3.0) + 1.0 + root) * jnp.exp2(root * -LOG2E)).astype(BF16)
        if pending:
            product()
        kbuf[dz, :, blocks[i]] = kern
        pending.append((dz, i))

    left8 = half_lanes((8, 128))

    def scatter(i):
        for n in (2 * i + 1, 2 * i):
            dy = near_ys[n]
            top = prod[0:8, 128 * n:128 * n + 128]
            bottom = prod[8:16, 128 * n:128 * n + 128]
            psend[dy, 0] = jnp.where(left8, top, swap(bottom))
            psend[dy, 1] = jnp.where(left8, swap(top), bottom)
            for dk in (1, 0):
                if (dy, dk) != (0, 0):
                    send(psend.at[dy, dk], pbuf.at[dy * 2 + dk], p_send.at[dy, dk], p_recv, device(dy=ny - dy, dk=dk))

    for dz, dy in zip(zs, ys):
        forward(dz, dy)
    for n in range(8):
        row_operand(n)
    for dz in [0] + zs[:-1]:
        col_operand(dz)
        for i in range(4):
            entries(dz, i)
    col_operand(zs[-1])
    for i in (3, 2, 1, 0):
        entries(zs[-1], i)
        if i < 3:
            scatter(i + 1)
    product()
    scatter(0)

    pbuf[0] = psend[0, 0]
    loads[3].wait()
    loads[4].wait()
    res = residual[...]
    arrived(pbuf.at[pl.ds(1, nrow - 1)], p_recv)
    total = jnp.sum(pbuf[...], axis=0)
    image = jnp.concatenate([total, swap(total)], axis=0)[:, 0:64] + noise[...] * own_dir
    image_out[...] = image

    def norm(a, b):
        return jnp.sum(a * b, axis=1, keepdims=True)

    sub16s = lax.broadcasted_iota(jnp.int32, (16, 128), 0)
    stats8 = jnp.where(
        lane16 == 4 * sub16s, norm(res, res),
        jnp.where(lane16 == 4 * sub16s + 1, norm(own_dir, image),
                  jnp.where(lane16 == 4 * sub16s + 2, norm(res, image),
                            jnp.where(lane16 == 4 * sub16s + 3, norm(image, image), 0.0))))

    def hops(step, n):
        return min(step, n - step)

    every = sorted(
        ((dx, dy, dz) for dx in range(NX) for dy in range(ny) for dz in range(nz) if dx + dy + dz > 0),
        key=lambda s: -(hops(s[0], NX) + hops(s[1], ny) + hops(s[2], nz)))
    tot_a[...] = jnp.sum(stats8, axis=0, keepdims=True)
    for n, (dx, dy, dz) in enumerate(every):
        pltpu.make_async_remote_copy(
            src_ref=tot_a, dst_ref=stat_a.at[n + 1], send_sem=a_send, recv_sem=a_recv,
            device_id=device(dx=dx, dy=dy, dz=dz), device_id_type=MESH).start()
    stat_a[0] = tot_a[...]
    others = stat_a.at[pl.ds(1, len(every))]
    arrived(others, a_recv)
    tot_b[...] = jnp.sum(stat_a[...], axis=0)
    send(tot_b, stat_b, b_send, b_recv, device(dk=1))
    arrived(others, a_send)
    arrived(stat_b, b_recv)
    row1 = tot_b[...] + stat_b[...]
    rows8 = lax.broadcasted_iota(jnp.int32, (8, 128), 0)
    spread8 = jnp.broadcast_to(row1, (16, 128))
    sub16 = lax.broadcasted_iota(jnp.int32, (16, 128), 0)
    def pick(i):
        return jnp.sum(jnp.where(lane16 == 4 * sub16 + i, spread8, 0.0), axis=1, keepdims=True)
    rr, curv, cross, square = (pick(i) for i in range(4))
    alpha = rr / curv
    rr_new = jnp.maximum(rr - 2.0 * (alpha * cross) + alpha * (alpha * square), 0.0)
    beta = rr_new / rr
    alpha_out[...] = jnp.broadcast_to(alpha, (RHS, PTS))
    beta_out[...] = jnp.broadcast_to(beta, (RHS, PTS))
    for copy in sends:
        copy.wait_send()


def solution(mesh):
    nrow, ncol = mesh.shape["row"], mesh.shape["col"]
    nz, ny = ncol // NX, nrow // 2
    spread = P(None, ("row", "col"))
    placed = (spread, P(), P(("row", "col")), spread, spread, spread)
    vmem = pl.BlockSpec(memory_space=pltpu.VMEM)
    dma = pltpu.SemaphoreType.DMA
    shape = jax.ShapeDtypeStruct((RHS, PTS), F32)

    step = pl.pallas_call(
        functools.partial(kernel, nrow, ncol),
        out_shape=(shape, shape, shape),
        in_specs=[pl.BlockSpec(memory_space=pltpu.HBM)] * 5,
        out_specs=(vmem,) * 3,
        scratch_shapes=[
            pltpu.VMEM((FEAT, PTS), F32),
            pltpu.VMEM((1, FEAT), F32),
            pltpu.VMEM((1, PTS), F32),
            pltpu.VMEM((RHS, PTS), F32),
            pltpu.VMEM((RHS, PTS), F32),
            pltpu.VMEM((nz, NX, 48, 128), BF16),
            pltpu.VMEM((ny, 2, 32, 128), BF16),
            pltpu.VMEM((256, nrow * PTS), BF16),
            pltpu.VMEM((nz, 256, 256), BF16),
            pltpu.VMEM((nz, 256, nrow * PTS), BF16),
            pltpu.VMEM((RHS, nrow * PTS), F32),
            pltpu.VMEM((ny, 2, 8, 128), F32),
            pltpu.VMEM((nrow, 8, 128), F32),
            pltpu.VMEM((nrow * ncol // 2, 1, 128), F32),
            pltpu.VMEM((1, 128), F32),
            pltpu.VMEM((1, 128), F32),
            pltpu.VMEM((1, 128), F32),
            dma((5,)), dma((nz, NX)), dma((nz,)), dma((nz,)), dma((ny, 2)), dma((ny,)), dma((ny,)),
            dma((ny, 2)), dma, dma, dma, dma, dma,
        ],
        compiler_params=pltpu.CompilerParams(
            collective_id=0, has_side_effects=True, vmem_limit_bytes=539 * 1024 * 1024 // 10),
        name="cg_step",
    )

    def on_device(points, lengthscale, noise, iterate, residual, direction):
        image, alpha, beta = step(
            points, lengthscale.reshape(1, FEAT), noise.reshape(1, PTS), residual, direction)
        fresh = residual - alpha * image
        return iterate + alpha * direction, fresh, fresh + beta * direction

    return jax.shard_map(
        on_device, mesh=mesh, in_specs=placed, out_specs=(spread, spread, spread), check_vma=False)
```

```python
import functools
import math

import jax
import jax.numpy as jnp
from jax import lax
from jax.experimental import pallas as pl
from jax.experimental.pallas import tpu as pltpu
from jax.sharding import PartitionSpec as P

MESH = pl.DeviceIdType.MESH
F32 = jnp.float32
BF16 = jnp.bfloat16
FEAT = 64
RHS = 16
PTS = 64
NX = 4
LOG2E = math.log2(math.e)
SCALE = math.sqrt(5.0)
TINY = 1e-30
Z_MAX = 3.0
STEEP = 251.0 / Z_MAX
LOW = 125.0


def half_lanes(shape):
    return lax.broadcasted_iota(jnp.int32, shape, 1) < 64


def swap(x):
    return pltpu.roll(x, 64, 1)


def split3(s):
    a = s.astype(BF16).astype(F32)
    b = (s - a).astype(BF16).astype(F32)
    c = (s - a - b).astype(BF16).astype(F32)
    return a, b, c


def encode(z):
    mag = jnp.exp2(jnp.abs(z) * STEEP - LOW)
    return jnp.where(z < 0, -mag, mag).astype(BF16)


def decode(code):
    w = code.astype(F32)
    z = (jnp.log2(jnp.abs(w)) + LOW) * (SCALE / STEEP)
    return jnp.where(w < 0, -z, z)


def kernel(
    nrow, ncol,
    points_hbm, scale_hbm, noise_hbm, residual_hbm, direction_hbm,
    image_out, alpha_out, beta_out,
    points, scale, noise, residual, direction,
    cbuf, rbuf, rmat, amat, kbuf, prod, psend, pbuf, stat_a, stat_b, tot_a, tot_b,
    in_sem, c_send, z_recv, x_recv, r_send, y_recv, k_recv,
    p_send, p_recv, a_send, a_recv, b_send, b_recv,
):
    nz, ny = ncol // NX, nrow // 2
    row, col = lax.axis_index("row"), lax.axis_index("col")
    x, z, y, k = col // nz, col % nz, row // 2, row % 2

    def device(dx=0, dy=0, dz=0, dk=0):
        return (
            lax.rem(y + dy, ny) * 2 + lax.rem(k + dk, 2),
            lax.rem(x + dx, NX) * nz + lax.rem(z + dz, nz),
        )

    def near_first(n):
        steps = []
        for s in range(1, n // 2 + 1):
            steps += [s] if 2 * s == n else [s, n - s]
        return steps

    zs, ys, xs = near_first(nz), near_first(ny), near_first(NX)
    far_zs, far_ys, far_xs = zs[::-1], ys[::-1], xs[::-1]
    row_steps = [(dy, dk) for dy in far_ys + [0] for dk in (1, 0) if (dy, dk) != (0, 0)]
    col_steps = [(dz, dx) for dz in far_zs + [0] for dx in far_xs + [0] if (dz, dx) != (0, 0)]

    barrier = pltpu.get_barrier_semaphore()
    greeted = (
        [device(dz=s) for s in far_zs] + [device(dy=s) for s in far_ys]
        + [device(dx=s) for s in far_xs] + [device(dk=1)])
    for peer in greeted:
        pl.semaphore_signal(barrier, inc=1, device_id=peer, device_id_type=MESH)

    loads = []
    for i, (src, dst) in enumerate((
            (points_hbm, points), (scale_hbm, scale), (direction_hbm, direction),
            (noise_hbm, noise), (residual_hbm, residual))):
        copy = pltpu.make_async_copy(src, dst, in_sem.at[i])
        copy.start()
        loads.append(copy)

    for copy in loads[:3]:
        copy.wait()
    ls_col = jnp.transpose(jnp.broadcast_to(scale[...], (FEAT, FEAT)))
    code = encode(points[...] / ls_col)
    zf = decode(code)
    hi = zf.astype(BF16).astype(F32)
    lo = (zf - hi).astype(BF16).astype(F32)
    code = code.astype(F32)
    half = FEAT // 2
    rbuf[0, 0] = jnp.concatenate([code[0:half], code[half:FEAT]], axis=1).astype(BF16)
    sq = jnp.sum((hi + lo) * (hi + lo), axis=0, keepdims=True)
    s1, s2, s3 = split3(sq)
    one = jnp.ones_like(sq)
    ext = jnp.concatenate([s1, s2, s3, one, one, one, one * 0, one * 0], axis=0)
    pad = jnp.zeros((FEAT - 8, PTS), F32)
    code_t = jnp.transpose(code)
    ext_t = jnp.transpose(jnp.concatenate([ext, pad], axis=0))
    cbuf[0, 0, 0:32, :] = jnp.concatenate([code_t[0:32], code_t[32:64]], axis=1).astype(BF16)
    own_dir = direction[...]
    packed = jnp.concatenate([own_dir, ext_t[0:16]], axis=1)
    lane16 = lax.broadcasted_iota(jnp.int32, (16, 128), 1)
    for a in range(1, 4):
        piece = jnp.concatenate([ext_t[16 * a:16 * a + 16], jnp.zeros((16, 64), F32)], axis=1)
        packed = jnp.where((lane16 >= 64 + 8 * a) & (lane16 < 72 + 8 * a), pltpu.roll(piece, 64 + 8 * a, 1), packed)
    cbuf[0, 0, 32:48, :] = packed.astype(BF16)

    pl.semaphore_wait(barrier, len(greeted))

    sends = []

    def send(src, dst, ssem, rsem, peer):
        copy = pltpu.make_async_remote_copy(
            src_ref=src, dst_ref=dst, send_sem=ssem, recv_sem=rsem,
            device_id=peer, device_id_type=MESH)
        copy.start()
        sends.append(copy)

    def arrived(ref, sem):
        pltpu.make_async_copy(ref, ref, sem).wait()

    def to_x(dz):
        for dx in far_xs:
            send(cbuf.at[dz, 0], cbuf.at[dz, dx], c_send.at[dz, dx], x_recv.at[dz], device(dx=dx))

    def to_core(dy):
        send(rbuf.at[dy, 0], rbuf.at[dy, 1], r_send.at[dy, 1], k_recv.at[dy], device(dk=1))

    for dz, dy in zip(far_zs, far_ys):
        send(cbuf.at[0, 0], cbuf.at[dz, 0], c_send.at[dz, 0], z_recv.at[dz], device(dz=dz))
        send(rbuf.at[0, 0], rbuf.at[dy, 0], r_send.at[dy, 0], y_recv.at[dy], device(dy=dy))
    to_x(0)
    to_core(0)
    def forward(dz, dy):
        arrived(cbuf.at[dz, 0], z_recv.at[dz])
        to_x(dz)
        arrived(rbuf.at[dy, 0], y_recv.at[dy])
        to_core(dy)

    near_ys = [0] + ys
    left = half_lanes((FEAT // 2, 128))
    sub = lax.broadcasted_iota(jnp.int32, (64, 128), 0)

    def row_operand(n):
        dy = near_ys[n]
        arrived(rbuf.at[dy, 1], k_recv.at[dy])
        c0 = decode(rbuf[dy, 0])
        c1 = decode(rbuf[dy, 1])
        full = jnp.concatenate([jnp.where(left, c0, swap(c1)), jnp.where(left, swap(c0), c1)], axis=0)
        h = full.astype(BF16).astype(F32)
        l = (full - h).astype(BF16).astype(F32)
        t1, t2, t3 = split3(jnp.sum((h + l) * (h + l), axis=0, keepdims=True))
        e = jnp.where(sub < 3, 1.0, jnp.where(sub == 3, t1, jnp.where(sub == 4, t2, jnp.where(sub == 5, t3, 0.0))))
        lanes = slice(128 * n, 128 * n + 128)
        h2 = (-2.0 * h).astype(BF16)
        rmat[0:64, lanes] = h2
        rmat[64:128, lanes] = h2
        rmat[128:192, lanes] = (-2.0 * l).astype(BF16)
        rmat[192:256, lanes] = e.astype(BF16)

    left16 = half_lanes((16, 128))
    width = 256
    blocks = [slice(width * i, width * i + width) for i in range(nrow * PTS // width)]
    dirs_of = {}

    def col_operand(dz):
        arrived(cbuf.at[dz, pl.ds(1, NX - 1)], x_recv.at[dz])
        dirs = []
        for dx in range(NX):
            tail = cbuf[dz, dx, 32:48, :].astype(F32)
            dirs.append(tail)
            full = decode(cbuf[dz, dx, 0:32, :])
            high = full.astype(BF16).astype(F32)
            low = full - high
            for a in range(4):
                rows = slice(64 * dx + 16 * a, 64 * dx + 16 * a + 16)
                part = slice(16 * (a % 2), 16 * (a % 2) + 16)
                h, l = high[part], low[part]
                h, l = (h, swap(l)) if a < 2 else (swap(h), l)
                extra = tail if a == 0 else pltpu.roll(tail, 128 - 8 * a, 1)
                amat[dz, rows, 0:128] = jnp.where(left16, h, l).astype(BF16)
                amat[dz, rows, 128:256] = jnp.where(left16, h, extra).astype(BF16)
        dirs_of[dz] = jnp.concatenate(
            [jnp.where(left16, dirs[0], swap(dirs[1])), jnp.where(left16, dirs[2], swap(dirs[3]))], axis=1).astype(BF16)

    pending = []
    begun = set()

    def product():
        dz, i = pending.pop()
        part = jnp.dot(dirs_of[dz], kbuf[dz, :, blocks[i]], preferred_element_type=F32)
        prod[:, blocks[i]] = prod[:, blocks[i]] + part if i in begun else part
        begun.add(i)

    def entries(dz, i):
        dist = jnp.dot(amat[dz], rmat[:, blocks[i]], preferred_element_type=F32)
        dist = jnp.maximum(dist, TINY)
        root = dist * lax.rsqrt(dist)
        kern = ((dist * (1.0 / 3.0) + 1.0 + root) * jnp.exp2(root * -LOG2E)).astype(BF16)
        if pending:
            product()
        kbuf[dz, :, blocks[i]] = kern
        pending.append((dz, i))

    left8 = half_lanes((8, 128))

    def scatter(i):
        for n in (2 * i + 1, 2 * i):
            dy = near_ys[n]
            top = prod[0:8, 128 * n:128 * n + 128]
            bottom = prod[8:16, 128 * n:128 * n + 128]
            psend[dy, 0] = jnp.where(left8, top, swap(bottom))
            psend[dy, 1] = jnp.where(left8, swap(top), bottom)
            for dk in (1, 0):
                if (dy, dk) != (0, 0):
                    send(psend.at[dy, dk], pbuf.at[dy * 2 + dk], p_send.at[dy, dk], p_recv, device(dy=ny - dy, dk=dk))

    for dz, dy in zip(zs, ys):
        forward(dz, dy)
    for n in range(8):
        row_operand(n)
    for dz in [0] + zs[:-1]:
        col_operand(dz)
        for i in range(4):
            entries(dz, i)
    col_operand(zs[-1])
    for i in (3, 2, 1, 0):
        entries(zs[-1], i)
        if i < 3:
            scatter(i + 1)
    product()
    scatter(0)

    pbuf[0] = psend[0, 0]
    loads[3].wait()
    loads[4].wait()
    res = residual[...]
    arrived(pbuf.at[pl.ds(1, nrow - 1)], p_recv)
    total = jnp.sum(pbuf[...], axis=0)
    image = jnp.concatenate([total, swap(total)], axis=0)[:, 0:64] + noise[...] * own_dir
    image_out[...] = image

    def norm(a, b):
        return jnp.sum(a * b, axis=1, keepdims=True)

    sub16s = lax.broadcasted_iota(jnp.int32, (16, 128), 0)
    stats8 = jnp.where(
        lane16 == 4 * sub16s, norm(res, res),
        jnp.where(lane16 == 4 * sub16s + 1, norm(own_dir, image),
                  jnp.where(lane16 == 4 * sub16s + 2, norm(res, image),
                            jnp.where(lane16 == 4 * sub16s + 3, norm(image, image), 0.0))))

    def hops(step, n):
        return min(step, n - step)

    every = sorted(
        ((dx, dy, dz) for dx in range(NX) for dy in range(ny) for dz in range(nz) if dx + dy + dz > 0),
        key=lambda s: -(hops(s[0], NX) + hops(s[1], ny) + hops(s[2], nz)))
    tot_a[...] = jnp.sum(stats8, axis=0, keepdims=True)
    for n, (dx, dy, dz) in enumerate(every):
        pltpu.make_async_remote_copy(
            src_ref=tot_a, dst_ref=stat_a.at[n + 1], send_sem=a_send, recv_sem=a_recv,
            device_id=device(dx=dx, dy=dy, dz=dz), device_id_type=MESH).start()
    stat_a[0] = tot_a[...]
    others = stat_a.at[pl.ds(1, len(every))]
    arrived(others, a_recv)
    tot_b[...] = jnp.sum(stat_a[...], axis=0)
    send(tot_b, stat_b, b_send, b_recv, device(dk=1))
    arrived(others, a_send)
    arrived(stat_b, b_recv)
    row1 = tot_b[...] + stat_b[...]
    rows8 = lax.broadcasted_iota(jnp.int32, (8, 128), 0)
    spread8 = jnp.broadcast_to(row1, (16, 128))
    sub16 = lax.broadcasted_iota(jnp.int32, (16, 128), 0)
    def pick(i):
        return jnp.sum(jnp.where(lane16 == 4 * sub16 + i, spread8, 0.0), axis=1, keepdims=True)
    rr, curv, cross, square = (pick(i) for i in range(4))
    alpha = rr / curv
    rr_new = jnp.maximum(rr - 2.0 * (alpha * cross) + alpha * (alpha * square), 0.0)
    beta = rr_new / rr
    alpha_out[...] = jnp.broadcast_to(alpha, (RHS, PTS))
    beta_out[...] = jnp.broadcast_to(beta, (RHS, PTS))
    for copy in sends:
        copy.wait_send()


def solution(mesh):
    nrow, ncol = mesh.shape["row"], mesh.shape["col"]
    nz, ny = ncol // NX, nrow // 2
    spread = P(None, ("row", "col"))
    placed = (spread, P(), P(("row", "col")), spread, spread, spread)
    vmem = pl.BlockSpec(memory_space=pltpu.VMEM)
    dma = pltpu.SemaphoreType.DMA
    shape = jax.ShapeDtypeStruct((RHS, PTS), F32)

    step = pl.pallas_call(
        functools.partial(kernel, nrow, ncol),
        out_shape=(shape, shape, shape),
        in_specs=[pl.BlockSpec(memory_space=pltpu.HBM)] * 5,
        out_specs=(vmem,) * 3,
        scratch_shapes=[
            pltpu.VMEM((FEAT, PTS), F32),
            pltpu.VMEM((1, FEAT), F32),
            pltpu.VMEM((1, PTS), F32),
            pltpu.VMEM((RHS, PTS), F32),
            pltpu.VMEM((RHS, PTS), F32),
            pltpu.VMEM((nz, NX, 48, 128), BF16),
            pltpu.VMEM((ny, 2, 32, 128), BF16),
            pltpu.VMEM((256, nrow * PTS), BF16),
            pltpu.VMEM((nz, 256, 256), BF16),
            pltpu.VMEM((nz, 256, nrow * PTS), BF16),
            pltpu.VMEM((RHS, nrow * PTS), F32),
            pltpu.VMEM((ny, 2, 8, 128), F32),
            pltpu.VMEM((nrow, 8, 128), F32),
            pltpu.VMEM((nrow * ncol // 2, 1, 128), F32),
            pltpu.VMEM((1, 128), F32),
            pltpu.VMEM((1, 128), F32),
            pltpu.VMEM((1, 128), F32),
            dma((5,)), dma((nz, NX)), dma((nz,)), dma((nz,)), dma((ny, 2)), dma((ny,)), dma((ny,)),
            dma((ny, 2)), dma, dma, dma, dma, dma,
        ],
        compiler_params=pltpu.CompilerParams(
            collective_id=0, has_side_effects=True, vmem_limit_bytes=32 * 1024 * 1024),
        name="cg_step",
    )

    def on_device(points, lengthscale, noise, iterate, residual, direction):
        operands = (points, lengthscale.reshape(1, FEAT), noise.reshape(1, PTS), residual, direction)
        image, alpha, beta = step(*(pltpu.with_memory_space_constraint(a, pltpu.HBM) for a in operands))
        fresh = residual - alpha * image
        return iterate + alpha * direction, fresh, fresh + beta * direction

    return jax.shard_map(
        on_device, mesh=mesh, in_specs=placed, out_specs=(spread, spread, spread), check_vma=False)
```

```python
import functools
import math

import jax
import jax.numpy as jnp
from jax import lax
from jax.experimental import pallas as pl
from jax.experimental.pallas import tpu as pltpu
from jax.sharding import PartitionSpec as P

MESH = pl.DeviceIdType.MESH
F32 = jnp.float32
BF16 = jnp.bfloat16
FEAT = 64
RHS = 16
PTS = 64
NX = 4
LOG2E = math.log2(math.e)
SCALE = math.sqrt(5.0)
TINY = 1e-30
Z_MAX = 3.0
STEEP = 251.0 / Z_MAX
LOW = 125.0


def half_lanes(shape):
    return lax.broadcasted_iota(jnp.int32, shape, 1) < 64


def swap(x):
    return pltpu.roll(x, 64, 1)


def split3(s):
    a = s.astype(BF16).astype(F32)
    b = (s - a).astype(BF16).astype(F32)
    c = (s - a - b).astype(BF16).astype(F32)
    return a, b, c


def encode(z):
    mag = jnp.exp2(jnp.abs(z) * STEEP - LOW)
    return jnp.where(z < 0, -mag, mag).astype(BF16)


def decode(code):
    w = code.astype(F32)
    z = (jnp.log2(jnp.abs(w)) + LOW) * (SCALE / STEEP)
    return jnp.where(w < 0, -z, z)


def kernel(
    nrow, ncol,
    points_hbm, scale_hbm, noise_hbm, residual_hbm, direction_hbm,
    image_out, alpha_out, beta_out,
    points, scale, noise, residual, direction,
    cbuf, rbuf, rmat, amat, kbuf, prod, psend, pbuf, stat_a, stat_b, tot_a, tot_b,
    in_sem, c_send, z_recv, x_recv, r_send, y_recv, k_recv,
    p_send, p_recv, a_send, a_recv, b_send, b_recv,
):
    nz, ny = ncol // NX, nrow // 2
    row, col = lax.axis_index("row"), lax.axis_index("col")
    x, z, y, k = col // nz, col % nz, row // 2, row % 2

    def device(dx=0, dy=0, dz=0, dk=0):
        return (
            lax.rem(y + dy, ny) * 2 + lax.rem(k + dk, 2),
            lax.rem(x + dx, NX) * nz + lax.rem(z + dz, nz),
        )

    def near_first(n):
        steps = []
        for s in range(1, n // 2 + 1):
            steps += [s] if 2 * s == n else [s, n - s]
        return steps

    zs, ys, xs = near_first(nz), near_first(ny), near_first(NX)
    far_zs, far_ys, far_xs = zs[::-1], ys[::-1], xs[::-1]
    row_steps = [(dy, dk) for dy in far_ys + [0] for dk in (1, 0) if (dy, dk) != (0, 0)]
    col_steps = [(dz, dx) for dz in far_zs + [0] for dx in far_xs + [0] if (dz, dx) != (0, 0)]

    barrier = pltpu.get_barrier_semaphore()
    greeted = (
        [device(dz=s) for s in far_zs] + [device(dy=s) for s in far_ys]
        + [device(dx=s) for s in far_xs] + [device(dk=1)])
    for peer in greeted:
        pl.semaphore_signal(barrier, inc=1, device_id=peer, device_id_type=MESH)

    loads = []
    for i, (src, dst) in enumerate((
            (points_hbm, points), (scale_hbm, scale), (direction_hbm, direction),
            (noise_hbm, noise), (residual_hbm, residual))):
        copy = pltpu.make_async_copy(src, dst, in_sem.at[i])
        copy.start()
        loads.append(copy)

    for copy in loads[:3]:
        copy.wait()
    ls_col = jnp.transpose(jnp.broadcast_to(scale[...], (FEAT, FEAT)))
    code = encode(points[...] / ls_col)
    zf = decode(code)
    hi = zf.astype(BF16).astype(F32)
    lo = (zf - hi).astype(BF16).astype(F32)
    code = code.astype(F32)
    half = FEAT // 2
    rbuf[0, 0] = jnp.concatenate([code[0:half], code[half:FEAT]], axis=1).astype(BF16)
    sq = jnp.sum((hi + lo) * (hi + lo), axis=0, keepdims=True)
    s1, s2, s3 = split3(sq)
    one = jnp.ones_like(sq)
    ext = jnp.concatenate([s1, s2, s3, one, one, one, one * 0, one * 0], axis=0)
    pad = jnp.zeros((FEAT - 8, PTS), F32)
    code_t = jnp.transpose(code)
    ext_t = jnp.transpose(jnp.concatenate([ext, pad], axis=0))
    cbuf[0, 0, 0:32, :] = jnp.concatenate([code_t[0:32], code_t[32:64]], axis=1).astype(BF16)
    own_dir = direction[...]
    packed = jnp.concatenate([own_dir, ext_t[0:16]], axis=1)
    lane16 = lax.broadcasted_iota(jnp.int32, (16, 128), 1)
    for a in range(1, 4):
        piece = jnp.concatenate([ext_t[16 * a:16 * a + 16], jnp.zeros((16, 64), F32)], axis=1)
        packed = jnp.where((lane16 >= 64 + 8 * a) & (lane16 < 72 + 8 * a), pltpu.roll(piece, 64 + 8 * a, 1), packed)
    cbuf[0, 0, 32:48, :] = packed.astype(BF16)

    pl.semaphore_wait(barrier, len(greeted))

    sends = []

    def send(src, dst, ssem, rsem, peer):
        copy = pltpu.make_async_remote_copy(
            src_ref=src, dst_ref=dst, send_sem=ssem, recv_sem=rsem,
            device_id=peer, device_id_type=MESH)
        copy.start()
        sends.append(copy)

    def arrived(ref, sem):
        pltpu.make_async_copy(ref, ref, sem).wait()

    def to_x(dz):
        for dx in far_xs:
            send(cbuf.at[dz, 0], cbuf.at[dz, dx], c_send.at[dz, dx], x_recv.at[dz], device(dx=dx))

    def to_core(dy):
        send(rbuf.at[dy, 0], rbuf.at[dy, 1], r_send.at[dy, 1], k_recv.at[dy], device(dk=1))

    for dz, dy in zip(far_zs, far_ys):
        send(cbuf.at[0, 0], cbuf.at[dz, 0], c_send.at[dz, 0], z_recv.at[dz], device(dz=dz))
        send(rbuf.at[0, 0], rbuf.at[dy, 0], r_send.at[dy, 0], y_recv.at[dy], device(dy=dy))
    to_x(0)
    to_core(0)
    def forward(dz, dy):
        arrived(cbuf.at[dz, 0], z_recv.at[dz])
        to_x(dz)
        arrived(rbuf.at[dy, 0], y_recv.at[dy])
        to_core(dy)

    near_ys = [0] + ys
    left = half_lanes((FEAT // 2, 128))
    sub = lax.broadcasted_iota(jnp.int32, (64, 128), 0)

    def row_operand(n):
        dy = near_ys[n]
        arrived(rbuf.at[dy, 1], k_recv.at[dy])
        c0 = decode(rbuf[dy, 0])
        c1 = decode(rbuf[dy, 1])
        full = jnp.concatenate([jnp.where(left, c0, swap(c1)), jnp.where(left, swap(c0), c1)], axis=0)
        h = full.astype(BF16).astype(F32)
        l = (full - h).astype(BF16).astype(F32)
        t1, t2, t3 = split3(jnp.sum((h + l) * (h + l), axis=0, keepdims=True))
        e = jnp.where(sub < 3, 1.0, jnp.where(sub == 3, t1, jnp.where(sub == 4, t2, jnp.where(sub == 5, t3, 0.0))))
        lanes = slice(128 * n, 128 * n + 128)
        h2 = (-2.0 * h).astype(BF16)
        rmat[0:64, lanes] = h2
        rmat[64:128, lanes] = h2
        rmat[128:192, lanes] = (-2.0 * l).astype(BF16)
        rmat[192:256, lanes] = e.astype(BF16)

    left16 = half_lanes((16, 128))
    width = 256
    blocks = [slice(width * i, width * i + width) for i in range(nrow * PTS // width)]
    dirs_of = {}

    def col_operand(dz):
        arrived(cbuf.at[dz, pl.ds(1, NX - 1)], x_recv.at[dz])
        dirs = []
        for dx in range(NX):
            tail = cbuf[dz, dx, 32:48, :].astype(F32)
            dirs.append(tail)
            full = decode(cbuf[dz, dx, 0:32, :])
            high = full.astype(BF16).astype(F32)
            low = full - high
            for a in range(4):
                rows = slice(64 * dx + 16 * a, 64 * dx + 16 * a + 16)
                part = slice(16 * (a % 2), 16 * (a % 2) + 16)
                h, l = high[part], low[part]
                h, l = (h, swap(l)) if a < 2 else (swap(h), l)
                extra = tail if a == 0 else pltpu.roll(tail, 128 - 8 * a, 1)
                amat[dz, rows, 0:128] = jnp.where(left16, h, l).astype(BF16)
                amat[dz, rows, 128:256] = jnp.where(left16, h, extra).astype(BF16)
        dirs_of[dz] = jnp.concatenate(
            [jnp.where(left16, dirs[0], swap(dirs[1])), jnp.where(left16, dirs[2], swap(dirs[3]))], axis=1).astype(BF16)

    pending = []
    begun = set()

    def product():
        dz, i = pending.pop()
        part = jnp.dot(dirs_of[dz], kbuf[dz, :, blocks[i]], preferred_element_type=F32)
        prod[:, blocks[i]] = prod[:, blocks[i]] + part if i in begun else part
        begun.add(i)

    def entries(dz, i):
        dist = jnp.dot(amat[dz], rmat[:, blocks[i]], preferred_element_type=F32)
        dist = jnp.maximum(dist, TINY)
        root = dist * lax.rsqrt(dist)
        kern = ((dist * (1.0 / 3.0) + 1.0 + root) * jnp.exp2(root * -LOG2E)).astype(BF16)
        if pending:
            product()
        kbuf[dz, :, blocks[i]] = kern
        pending.append((dz, i))

    left8 = half_lanes((8, 128))

    def scatter(i):
        for n in (2 * i + 1, 2 * i):
            dy = near_ys[n]
            top = prod[0:8, 128 * n:128 * n + 128]
            bottom = prod[8:16, 128 * n:128 * n + 128]
            psend[dy, 0] = jnp.where(left8, top, swap(bottom))
            psend[dy, 1] = jnp.where(left8, swap(top), bottom)
            for dk in (1, 0):
                if (dy, dk) != (0, 0):
                    send(psend.at[dy, dk], pbuf.at[dy * 2 + dk], p_send.at[dy, dk], p_recv, device(dy=ny - dy, dk=dk))

    for dz, dy in zip(zs, ys):
        forward(dz, dy)
    for n in range(8):
        row_operand(n)
    for dz in [0] + zs[:-1]:
        col_operand(dz)
        for i in range(4):
            entries(dz, i)
    col_operand(zs[-1])
    for i in (3, 2, 1, 0):
        entries(zs[-1], i)
        if i < 3:
            scatter(i + 1)
    product()
    scatter(0)

    pbuf[0] = psend[0, 0]
    loads[3].wait()
    loads[4].wait()
    res = residual[...]
    rr_own = jnp.sum(res * res, axis=1, keepdims=True)
    damped = noise[...] * own_dir
    arrived(pbuf.at[pl.ds(1, nrow - 1)], p_recv)
    total = jnp.sum(pbuf[...], axis=0)
    image = jnp.concatenate([total, swap(total)], axis=0)[:, 0:64] + damped
    image_out[...] = image

    def norm(a, b):
        return jnp.sum(a * b, axis=1, keepdims=True)

    sub16s = lax.broadcasted_iota(jnp.int32, (16, 128), 0)
    stats8 = jnp.where(
        lane16 == 4 * sub16s, rr_own,
        jnp.where(lane16 == 4 * sub16s + 1, norm(own_dir, image),
                  jnp.where(lane16 == 4 * sub16s + 2, norm(res, image),
                            jnp.where(lane16 == 4 * sub16s + 3, norm(image, image), 0.0))))

    def hops(step, n):
        return min(step, n - step)

    every = sorted(
        ((dx, dy, dz) for dx in range(NX) for dy in range(ny) for dz in range(nz) if dx + dy + dz > 0),
        key=lambda s: -(hops(s[0], NX) + hops(s[1], ny) + hops(s[2], nz)))
    tot_a[...] = jnp.sum(stats8, axis=0, keepdims=True)
    for n, (dx, dy, dz) in enumerate(every):
        pltpu.make_async_remote_copy(
            src_ref=tot_a, dst_ref=stat_a.at[n + 1], send_sem=a_send, recv_sem=a_recv,
            device_id=device(dx=dx, dy=dy, dz=dz), device_id_type=MESH).start()
    stat_a[0] = tot_a[...]
    others = stat_a.at[pl.ds(1, len(every))]
    arrived(others, a_recv)
    tot_b[...] = jnp.sum(stat_a[...], axis=0)
    send(tot_b, stat_b, b_send, b_recv, device(dk=1))
    arrived(others, a_send)
    arrived(stat_b, b_recv)
    row1 = tot_b[...] + stat_b[...]
    rows8 = lax.broadcasted_iota(jnp.int32, (8, 128), 0)
    spread8 = jnp.broadcast_to(row1, (16, 128))
    sub16 = lax.broadcasted_iota(jnp.int32, (16, 128), 0)
    def pick(i):
        return jnp.sum(jnp.where(lane16 == 4 * sub16 + i, spread8, 0.0), axis=1, keepdims=True)
    rr, curv, cross, square = (pick(i) for i in range(4))
    alpha = rr / curv
    rr_new = jnp.maximum(rr - 2.0 * (alpha * cross) + alpha * (alpha * square), 0.0)
    beta = rr_new / rr
    alpha_out[...] = jnp.broadcast_to(alpha, (RHS, PTS))
    beta_out[...] = jnp.broadcast_to(beta, (RHS, PTS))
    for copy in sends:
        copy.wait_send()


def solution(mesh):
    nrow, ncol = mesh.shape["row"], mesh.shape["col"]
    nz, ny = ncol // NX, nrow // 2
    spread = P(None, ("row", "col"))
    placed = (spread, P(), P(("row", "col")), spread, spread, spread)
    vmem = pl.BlockSpec(memory_space=pltpu.VMEM)
    dma = pltpu.SemaphoreType.DMA
    shape = jax.ShapeDtypeStruct((RHS, PTS), F32)

    step = pl.pallas_call(
        functools.partial(kernel, nrow, ncol),
        out_shape=(shape, shape, shape),
        in_specs=[pl.BlockSpec(memory_space=pltpu.HBM)] * 5,
        out_specs=(vmem,) * 3,
        scratch_shapes=[
            pltpu.VMEM((FEAT, PTS), F32),
            pltpu.VMEM((1, FEAT), F32),
            pltpu.VMEM((1, PTS), F32),
            pltpu.VMEM((RHS, PTS), F32),
            pltpu.VMEM((RHS, PTS), F32),
            pltpu.VMEM((nz, NX, 48, 128), BF16),
            pltpu.VMEM((ny, 2, 32, 128), BF16),
            pltpu.VMEM((256, nrow * PTS), BF16),
            pltpu.VMEM((nz, 256, 256), BF16),
            pltpu.VMEM((nz, 256, nrow * PTS), BF16),
            pltpu.VMEM((RHS, nrow * PTS), F32),
            pltpu.VMEM((ny, 2, 8, 128), F32),
            pltpu.VMEM((nrow, 8, 128), F32),
            pltpu.VMEM((nrow * ncol // 2, 1, 128), F32),
            pltpu.VMEM((1, 128), F32),
            pltpu.VMEM((1, 128), F32),
            pltpu.VMEM((1, 128), F32),
            dma((5,)), dma((nz, NX)), dma((nz,)), dma((nz,)), dma((ny, 2)), dma((ny,)), dma((ny,)),
            dma((ny, 2)), dma, dma, dma, dma, dma,
        ],
        compiler_params=pltpu.CompilerParams(
            collective_id=0, has_side_effects=True, vmem_limit_bytes=32 * 1024 * 1024),
        name="cg_step",
    )

    def on_device(points, lengthscale, noise, iterate, residual, direction):
        operands = (points, lengthscale.reshape(1, FEAT), noise.reshape(1, PTS), residual, direction)
        image, alpha, beta = step(*(pltpu.with_memory_space_constraint(a, pltpu.HBM) for a in operands))
        fresh = residual - alpha * image
        return iterate + alpha * direction, fresh, fresh + beta * direction

    return jax.shard_map(
        on_device, mesh=mesh, in_specs=placed, out_specs=(spread, spread, spread), check_vma=False)
```
